32 devices in a mesh: ep: 16 (over z, x, core), etp: 2 (over y).
Axes of the slice: x: 2, y: 2, z: 4, core: 2. Of those that a mesh axis runs over, the one named last changes fastest.
Arguments:
- tokens: bfloat16 [2048, 4096], P('ep', 'etp'), may hold values from -6 to 6
- cotangent: bfloat16 [2048, 4096], P('ep', 'etp'), may hold values from -0.29882812 to 0.29882812
- expert_ids: int32 [2048, 8], P('ep'), may hold values from 0 to 15, as said below
- slot_pos: int32 [2048, 8], P('ep'), may hold values from 0 to 79, as said below
- weights_prob: bfloat16 [2048, 8], P('ep'), may hold values from 0.049804688 to 1
- gate_proj: bfloat16 [16, 1536, 4096], P('ep', None, 'etp'), may hold values from -0.09375 to 0.09375
- up_proj: bfloat16 [16, 1536, 4096], P('ep', None, 'etp'), may hold values from -0.09375 to 0.09375
- down_proj: bfloat16 [16, 1536, 4096], P('ep', None, 'etp'), may hold values from -0.15625 to 0.15625
Outputs:
- grad_gate: bfloat16 [16, 1536, 4096], P('ep', 'etp')
- grad_up: bfloat16 [16, 1536, 4096], P('ep', 'etp')
- grad_down: bfloat16 [16, 1536, 4096], P('ep', 'etp')
- grad_probs: float32 [2048, 8], P('ep')
The draws below stay inside these ranges and needn't reach their ends.
Inputs may be any that keep to these rules, and one draw needn't show every extreme that they name: `expert_ids`: each row names 8 different experts. Within the 128 rows of one index of ep no expert is named more than 80 times, and one expert is named exactly 80 times in every such block; every expert is named somewhere. `slot_pos`: within the rows of one index of ep, the choices that name the same expert have different slots.
All inputs are finite; a program needn't handle non-finite values.
Results may differ from the reference program's by a relative error of at most 0.0058.
Values may be sent and summed in bfloat16 or wider, within the bound.
A program may use at most 192 MiB of HBM per device.

```python
import math
import jax
import jax.numpy as jnp
from jax import lax

D = 4096
FF = 1536
TOP = 8
TOK_DEV = 128
EXPERTS = 16
TOKENS = 2048
CAP = 80
ROWS = 1280


def assignment_tables(key):
    blocks = TOKENS // TOK_DEV
    assigned = TOK_DEV * TOP
    hot_count = EXPERTS // 4
    hot_tickets = hot_count * CAP
    rest_tickets = assigned - hot_tickets
    rest_ranks = EXPERTS - hot_count
    favored = jax.random.randint(jax.random.fold_in(key, 5), (), 0, EXPERTS)
    block_keys = jax.random.split(jax.random.fold_in(key, 9), blocks)

    def one_block(block_key):
        key_rank, key_perm, key_shift, key_turn = jax.random.split(block_key, 4)
        scores = jax.random.permutation(key_rank, EXPERTS).astype(jnp.int32)
        scores = jnp.where(jnp.arange(EXPERTS, dtype=jnp.int32) == favored, -1, scores)
        ranked = jnp.argsort(scores, stable=True).astype(jnp.int32)
        ticket = jnp.arange(assigned, dtype=jnp.int32)
        rest_offset = jnp.maximum(ticket - hot_tickets, 0)
        rest_rank = hot_count + rest_offset * rest_ranks // rest_tickets
        ranking = jnp.where(ticket < hot_tickets, ticket // CAP, rest_rank)
        rest_first = hot_tickets + ((ranking - hot_count) * rest_tickets + rest_ranks - 1) // rest_ranks
        first_ticket = jnp.where(ticket < hot_tickets, ranking * CAP, rest_first)
        expert_of = ranked[ranking]
        slot_shift = jax.random.randint(key_shift, (EXPERTS,), 0, CAP)
        slot_of = (ticket - first_ticket + slot_shift[expert_of]) % CAP
        ids_grid = expert_of.reshape(TOP, TOK_DEV).T
        slot_grid = slot_of.reshape(TOP, TOK_DEV).T
        token_order = jax.random.permutation(key_perm, TOK_DEV)
        rotation = jax.random.randint(key_turn, (TOK_DEV, 1), 0, TOP)
        columns = (jnp.arange(TOP, dtype=jnp.int32)[None, :] + rotation) % TOP
        ids_grid = jnp.take_along_axis(ids_grid[token_order], columns, axis=1)
        slot_grid = jnp.take_along_axis(slot_grid[token_order], columns, axis=1)
        return (ids_grid, slot_grid)
    ids_all, slots_all = jax.vmap(one_block)(block_keys)
    return (ids_all.reshape(TOKENS, TOP).astype(jnp.int32), slots_all.reshape(TOKENS, TOP).astype(jnp.int32))


def draw_expert_ids(key, part):
    return assignment_tables(jax.random.fold_in(key, 3))[0]


def draw_slot_pos(key, part):
    return assignment_tables(jax.random.fold_in(key, 3))[1]


def level_of(stream_key, dims, cuts, least, high):
    def one(dim, shards_of):
        steps = jax.random.uniform(jax.random.fold_in(jax.random.fold_in(stream_key, 6), dim), (shards_of,), jnp.float32, least / len(cuts), high / len(cuts))
        return jnp.repeat(jnp.exp(steps), dims[dim] // shards_of).reshape((-1,) + (1,) * (len(dims) - dim - 1))

    gain = one(*cuts[0])
    for cut in cuts[1:]:
        gain = gain * one(*cut)
    return gain


def normal_values(rng, shape, spread, reach, shards=(), held_as=jnp.bfloat16):
    result = jax.random.normal(rng, shape, jnp.float32) * spread
    if len(shards) > 0:
        result = level_of(rng, shape, shards, -0.22, 0.18) * result
    return jnp.clip(result, min=-reach, max=reach).astype(held_as)


def setup_inputs(seed: int = 0) -> dict:
    key_of = jax.random.split(jax.random.key(seed), 9)
    tokens = normal_values(key_of[0], (TOKENS, D), 1.0, 6.0, ((0, 16), (1, 2)))
    cotangent = normal_values(key_of[1], (TOKENS, D), 0.05, 0.29882812, ((0, 16), (1, 2)))
    expert_ids = draw_expert_ids(jax.random.fold_in(key_of[8], 71), 0)
    slot_pos = draw_slot_pos(jax.random.fold_in(key_of[8], 71), 0)
    weights_prob = jnp.clip(jnp.exp(math.log(1.0) - 2.9996462 * jax.random.uniform(key_of[4], (TOKENS, TOP), jnp.float32) ** level_of(key_of[4], (TOKENS, TOP), ((0, 16),), -0.2, 0.2)), 0.049804688, 1.0).astype(jnp.bfloat16)
    gate_proj = normal_values(key_of[5], (EXPERTS, FF, D), D ** -0.5, 0.09375, ((0, 16), (2, 2)))
    up_proj = normal_values(key_of[6], (EXPERTS, FF, D), D ** -0.5, 0.09375, ((0, 16), (2, 2)))
    down_proj = normal_values(key_of[7], (EXPERTS, FF, D), FF ** -0.5, 0.15625, ((0, 16), (2, 2)))
    return dict(tokens=tokens, cotangent=cotangent, expert_ids=expert_ids, slot_pos=slot_pos, weights_prob=weights_prob, gate_proj=gate_proj, up_proj=up_proj, down_proj=down_proj)


def reference(tokens, cotangent, expert_ids, slot_pos, weights_prob, gate_proj, up_proj, down_proj):
    assigned = TOKENS * TOP
    block_of = (jnp.arange(TOKENS, dtype=jnp.int32) // TOK_DEV)[:, None]
    flat_slot = (expert_ids * ROWS + block_of * CAP + slot_pos).reshape(-1).astype(jnp.int32)
    source = jnp.full((EXPERTS * ROWS,), assigned, jnp.int32)
    source = source.at[flat_slot].set(jnp.arange(assigned, dtype=jnp.int32)).reshape(EXPERTS, ROWS)
    padded_x = jnp.concatenate([tokens, jnp.zeros((1, D), tokens.dtype)], axis=0)
    padded_dy = jnp.concatenate([cotangent, jnp.zeros((1, D), cotangent.dtype)], axis=0)
    padded_prob = jnp.concatenate([weights_prob.reshape(-1), jnp.zeros((1,), weights_prob.dtype)], axis=0)

    def one_expert(expert):
        picked = source[expert]
        token_of = jnp.where(picked < assigned, picked // TOP, TOKENS).astype(jnp.int32)
        x_rows = padded_x[token_of]
        dy_rows = padded_dy[token_of]
        p_rows = padded_prob[picked].astype(jnp.float32)[:, None]
        gate_mat = gate_proj[expert]
        up_mat = up_proj[expert]
        down_mat = down_proj[expert]
        gate = jnp.dot(x_rows, gate_mat.T, preferred_element_type=jnp.float32)
        up_val = jnp.dot(x_rows, up_mat.T, preferred_element_type=jnp.float32)
        sigmoid_gate = jax.nn.sigmoid(gate)
        silu_gate = gate * sigmoid_gate
        hidden = (silu_gate * up_val).astype(jnp.bfloat16)
        probe = jnp.dot(dy_rows, down_mat.T, preferred_element_type=jnp.float32)
        row_probe = jnp.sum(hidden.astype(jnp.float32) * probe, axis=1)
        scaled_hidden = (p_rows * hidden.astype(jnp.float32)).astype(jnp.bfloat16)
        grad_down = jnp.dot(scaled_hidden.T, dy_rows, preferred_element_type=jnp.float32).astype(jnp.bfloat16)
        delta = p_rows * probe
        d_gate = (delta * up_val * sigmoid_gate * (1.0 + gate * (1.0 - sigmoid_gate))).astype(jnp.bfloat16)
        d_up = (delta * silu_gate).astype(jnp.bfloat16)
        grad_gate = jnp.dot(d_gate.T, x_rows, preferred_element_type=jnp.float32).astype(jnp.bfloat16)
        grad_up = jnp.dot(d_up.T, x_rows, preferred_element_type=jnp.float32).astype(jnp.bfloat16)
        return grad_gate, grad_up, grad_down, row_probe

    grad_gate, grad_up, grad_down, row_probe = lax.map(one_expert, jnp.arange(EXPERTS, dtype=jnp.int32))
    grad_probs = row_probe.reshape(-1)[flat_slot].reshape(TOKENS, TOP)
    return grad_gate, grad_up, grad_down, grad_probs
```

```python
import jax
import jax.numpy as jnp
from jax import lax
from jax.sharding import PartitionSpec as P


def local(tokens, cotangent, expert_ids, slot_pos, weights_prob, gate_proj, up_proj, down_proj):
    f32 = jnp.float32
    bf16 = jnp.bfloat16
    tok_rows, part_width = tokens.shape
    top_count = expert_ids.shape[1]
    ep_count = lax.axis_size("ep")
    etp_count = lax.axis_size("etp")
    my_ep = lax.axis_index("ep")
    my_etp = lax.axis_index("etp")
    slot_cap = 5 * tok_rows * top_count // (4 * ep_count)
    hidden_width = gate_proj.shape[1] // etp_count

    choices = jnp.concatenate(
        [expert_ids.astype(f32).T, slot_pos.astype(f32).T, weights_prob.astype(f32).T], axis=0
    )
    choices = lax.all_gather(choices, "ep", axis=0, tiled=False)
    named = choices[:, :top_count] == my_ep.astype(f32)
    slot_of = jnp.sum(
        jnp.where(named, choices[:, top_count : 2 * top_count] + 1.0, 0.0), axis=1
    )
    prob_of = jnp.sum(jnp.where(named, choices[:, 2 * top_count :], 0.0), axis=1)
    slot_index = lax.broadcasted_iota(jnp.int32, (ep_count, slot_cap, tok_rows), 1)
    taken = slot_of.astype(jnp.int32)[:, None, :] == slot_index + 1
    p_rows = jnp.sum(jnp.where(taken, prob_of[:, None, :], 0.0), axis=2).reshape(-1)[:, None]
    picker = taken.astype(bf16)

    def moved(values, step):
        perm = [(i, (i + step) % etp_count) for i in range(etp_count)]
        return lax.ppermute(values, "etp", perm)

    def origin_of(step):
        return (my_etp + etp_count - step) % etp_count

    x_parts = [tokens] + [moved(tokens, step) for step in range(1, etp_count)]
    dy_parts = [cotangent] + [moved(cotangent, step) for step in range(1, etp_count)]
    (x_tail, dy_tail, gate_proj, up_proj, down_proj) = lax.optimization_barrier(
        (x_parts[1:], dy_parts[1:], gate_proj, up_proj, down_proj)
    )
    x_parts = [tokens] + list(x_tail)
    dy_parts = [cotangent] + list(dy_tail)

    def blocks_of(parts):
        return [lax.all_gather(part, "ep", axis=0, tiled=False) for part in parts]

    x_blocks = blocks_of(x_parts)
    dy_blocks = blocks_of(dy_parts)

    def rows_of(values):
        rows = jnp.einsum("bst,btd->bsd", picker, values, preferred_element_type=f32)
        return rows.astype(bf16).reshape(ep_count * slot_cap, values.shape[2])

    def pieces(proj):
        mat = proj[0]
        out = []
        for step in range(etp_count):
            to = (my_etp + step) % etp_count
            piece = lax.dynamic_slice_in_dim(mat, to * hidden_width, hidden_width, axis=0)
            if step > 0:
                piece = moved(piece, step)
            out.append(piece)
        return out

    gate_pieces = pieces(gate_proj)
    up_pieces = pieces(up_proj)
    down_pieces = pieces(down_proj)

    def product(rows, mat):
        return jnp.einsum("rd,fd->rf", rows, mat, preferred_element_type=f32)

    def joined(parts):
        rows = jnp.zeros((parts[0].shape[0], part_width * etp_count), bf16)
        for step, part in enumerate(parts):
            rows = lax.dynamic_update_slice_in_dim(
                rows, part, origin_of(step) * part_width, axis=1
            )
        return rows

    gate = None
    up_val = None
    probe = None
    x_list = []
    dy_list = []
    for step in range(etp_count):
        part = rows_of(x_blocks[step])
        x_list.append(part)
        gate_term = product(part, gate_pieces[step])
        up_term = product(part, up_pieces[step])
        gate = gate_term if gate is None else gate + gate_term
        up_val = up_term if up_val is None else up_val + up_term
        if step + 1 < etp_count:
            x_blocks[step + 1], gate, up_val = lax.optimization_barrier(
                (x_blocks[step + 1], gate, up_val)
            )
    x_rows = joined(x_list)
    dy_blocks[0], gate, up_val, x_rows = lax.optimization_barrier(
        (dy_blocks[0], gate, up_val, x_rows)
    )
    sigmoid_gate = jax.nn.sigmoid(gate)
    silu_gate = gate * sigmoid_gate
    hidden = (silu_gate * up_val).astype(bf16)
    scaled_hidden = (p_rows * hidden.astype(f32)).astype(bf16)

    for step in range(etp_count):
        part = rows_of(dy_blocks[step])
        dy_list.append(part)
        term = product(part, down_pieces[step])
        probe = term if probe is None else probe + term
        if step + 1 < etp_count:
            dy_blocks[step + 1], probe, scaled_hidden = lax.optimization_barrier(
                (dy_blocks[step + 1], probe, scaled_hidden)
            )
    dy_rows = joined(dy_list)
    partial_probe = jnp.sum(hidden.astype(f32) * probe, axis=1)
    mine = lax.all_to_all(
        partial_probe.reshape(ep_count, slot_cap), "ep", split_axis=0, concat_axis=0, tiled=True
    )
    others = [moved(mine, step) for step in range(1, etp_count)]
    for other in others:
        mine = mine + other

    delta = p_rows * probe
    d_gate = (delta * up_val * sigmoid_gate * (1.0 + gate * (1.0 - sigmoid_gate))).astype(bf16)
    d_up = (delta * silu_gate).astype(bf16)

    def outer(left, right):
        return jnp.einsum("rf,rd->fd", left, right, preferred_element_type=f32).astype(bf16)[None]

    grad_gate = outer(d_gate, x_rows)
    grad_up = outer(d_up, x_rows)
    grad_down = outer(scaled_hidden, dy_rows)

    flat_slot = expert_ids * slot_cap + slot_pos
    row_index = lax.broadcasted_iota(jnp.int32, flat_slot.shape + (ep_count * slot_cap,), 2)
    grad_probs = jnp.sum(
        jnp.where(flat_slot[:, :, None] == row_index, mine.reshape(1, 1, -1), 0.0), axis=2
    )
    return (grad_gate, grad_up, grad_down, grad_probs)


def solution(mesh):
    in_specs = (
        P("ep", "etp"),
        P("ep", "etp"),
        P("ep", None),
        P("ep", None),
        P("ep", None),
        P("ep", None, "etp"),
        P("ep", None, "etp"),
        P("ep", None, "etp"),
    )
    out_specs = (P("ep", "etp", None), P("ep", "etp", None), P("ep", "etp", None), P("ep", None))
    return jax.shard_map(local, mesh=mesh, in_specs=in_specs, out_specs=out_specs, check_vma=False)
```
